32 devices in a mesh: seq: 8 (over z, y), tp: 4 (over x, core).
Axes of the slice: x: 2, y: 2, z: 4, core: 2. Of those that a mesh axis runs over, the one named last changes fastest.
Arguments:
- layer_input: bfloat16 [8, 640, 768], P('seq', 'tp'), may hold values from -6 to 6
- cotangent: bfloat16 [8, 640, 768], P('seq', 'tp'), may hold values from -6 to 6
- seq_lengths: int32 [32], replicated, may hold values from 64 to 512, as said below
- seq_group: int32 [32], replicated, may hold values from 0 to 7, as said below
- norm1_gain: float32 [768], replicated, may hold values from 0.5 to 1.5
- w_qkv: float32 [3, 768, 768], replicated, may hold values from -0.21875 to 0.21875
- mix_logits: float32 [12, 12], replicated, may hold values from -3 to 3
- mix_weights: float32 [12, 12], replicated, may hold values from -1.75 to 1.75
- w_attn_out: float32 [768, 768], replicated, may hold values from -1 to 1
- norm2_gain: float32 [768], replicated, may hold values from 0.5 to 1.5
- w_up: float32 [768, 3072], P(None, 'tp'), may hold values from -0.21875 to 0.21875
- w_down: float32 [3072, 768], P('tp'), may hold values from -0.109375 to 0.109375
Outputs:
- block_out: bfloat16 [8, 640, 768], P('seq', 'tp')
- input_grad: float32 [8, 640, 768], P('seq', 'tp')
- grad_norm1: float32 [768], replicated
- grad_qkv: float32 [3, 768, 768], replicated
- grad_mix_logits: float32 [12, 12], replicated
- grad_mix_weights: float32 [12, 12], replicated
- grad_attn_out: float32 [768, 768], replicated
- grad_norm2: float32 [768], replicated
- grad_up: float32 [768, 3072], P(None, 'tp')
- grad_down: float32 [3072, 768], P('tp')
- qkv_rows: float32 [3, 768], replicated
- qkv_cols: float32 [3, 768], replicated
- out_rows: float32 [768], replicated
- out_cols: float32 [768], replicated
- up_rows: float32 [768], replicated
- up_cols: float32 [3072], P('tp')
- down_rows: float32 [3072], P('tp')
- down_cols: float32 [768], replicated
- new_qkv: float32 [3, 768, 768], replicated
- new_attn_out: float32 [768, 768], replicated
- new_up: float32 [768, 3072], P(None, 'tp')
- new_down: float32 [3072, 768], P('tp')
The draws below stay inside these ranges and needn't reach their ends.
Inputs may be any that keep to these rules, and one draw needn't show every extreme that they name: `seq_lengths`: each entry is 1, 2, 4 or 8 times 64; for every group g the entries k with seq_group[k] = g add up to 640. `seq_group`: every group is named by some entries.
All inputs are finite; a program needn't handle non-finite values.
Results may differ from the reference program's by a relative error of at most 0.012.
The reference program's roundings to bfloat16 on the way count: a program that leaves them out, or rounds other values in their place, can miss the bound.
Values may be sent and summed in bfloat16 or wider, within the bound.
No kernel may reach another device: no remote copies, remote signals or barrier semaphores. Data moves between devices by JAX's collectives and lax.ppermute only.
A program may use at most 384 MiB of HBM per device.

```python
import jax
import jax.numpy as jnp
from jax import lax

D = 768
HEADS = 12
HEAD_DIM = 64
FF = 3072
MINLEN = 64
GROUPS = 8
SHARDS = 4
GROUP_TOK = 640
TOK_DEV = 160
NSEQS = 32


recipe_units = ((8, 2, 4, 2, 1, 1, 1, 1), (8, 1, 1, 4, 2, 2, 1, 1))


recipe_slots = ((0, 0, 1, 1, 1, 1, 1, 1), (0, 0, 0, 1, 1, 1, 1, 1))


def sequence_table(key):
    pair_count = GROUPS // 2
    recipe_ids = jax.random.randint(jax.random.fold_in(key, 11), (pair_count,), 0, 2)
    group_order = jax.random.permutation(jax.random.fold_in(key, 12), GROUPS).astype(jnp.int32)
    unit_counts = jnp.array(recipe_units, dtype=jnp.int32)[recipe_ids]
    slot_ids = jnp.array(recipe_slots, dtype=jnp.int32)[recipe_ids]
    owners = group_order[2 * jnp.arange(pair_count, dtype=jnp.int32)[:, None] + slot_ids]
    shuffle = jax.random.permutation(jax.random.fold_in(key, 13), NSEQS).astype(jnp.int32)
    lengths = (unit_counts * MINLEN).reshape(-1)[shuffle]
    return (lengths.astype(jnp.int32), owners.reshape(-1)[shuffle].astype(jnp.int32))


def draw_seq_lengths(key, part):
    lengths, owners = sequence_table(key)
    return lengths


def draw_seq_group(key, part):
    lengths, owners = sequence_table(key)
    return owners


def levels(own_key, shape, cuts, low, high):
    def one(dim, blocks):
        draws = jax.random.uniform(jax.random.fold_in(jax.random.fold_in(own_key, 6), dim), (blocks,), jnp.float32, low / len(cuts), high / len(cuts))
        return jnp.repeat(jnp.exp(draws), shape[dim] // blocks).reshape((-1,) + (1,) * (len(shape) - dim - 1))

    loudness = one(*cuts[0])
    for cut in cuts[1:]:
        loudness = loudness * one(*cut)
    return loudness


def noise(stream_key, extent, spread, bound, shards=(), held_as=jnp.bfloat16):
    level = levels(stream_key, extent, shards, -0.22, 0.18) if shards else 1.0
    values = jax.random.normal(stream_key, extent, jnp.float32) * spread * level
    return jnp.minimum(jnp.maximum(values, -bound), bound).astype(held_as)


def setup_inputs(seed: int = 0) -> dict:
    keys = jax.random.split(jax.random.key(seed), 13)
    layer_input = noise(keys[0], (GROUPS, GROUP_TOK, D), 1.0, 6.0, ((0, 8), (1, 4)))
    cotangent = noise(keys[1], (GROUPS, GROUP_TOK, D), 1.0, 6.0, ((0, 8), (1, 4)))
    seq_lengths = draw_seq_lengths(jax.random.fold_in(keys[12], 71), 0)
    seq_group = draw_seq_group(jax.random.fold_in(keys[12], 71), 0)
    norm1_gain = jnp.clip(1.0 + 0.1 * jax.random.normal(keys[4], (D,), jnp.float32), 0.5, 1.5)
    w_qkv = noise(keys[5], (3, D, D), D ** -0.5, 0.21875, (), jnp.float32)
    mix_logits = noise(keys[6], (HEADS, HEADS), 4 ** -0.5, 3.0, (), jnp.float32)
    mix_weights = noise(keys[7], (HEADS, HEADS), HEADS ** -0.5, 1.75, (), jnp.float32)
    w_attn_out = noise(keys[8], (D, D), (D // 24) ** -0.5, 1.0, (), jnp.float32)
    norm2_gain = jnp.clip(1.0 + 0.1 * jax.random.normal(keys[9], (D,), jnp.float32), 0.5, 1.5)
    w_up = noise(keys[10], (D, FF), D ** -0.5, 0.21875, ((1, 4),), jnp.float32)
    w_down = noise(keys[11], (FF, D), FF ** -0.5, 0.109375, ((0, 4),), jnp.float32)
    return {"layer_input": layer_input, "cotangent": cotangent, "seq_lengths": seq_lengths, "seq_group": seq_group, "norm1_gain": norm1_gain, "w_qkv": w_qkv, "mix_logits": mix_logits, "mix_weights": mix_weights, "w_attn_out": w_attn_out, "norm2_gain": norm2_gain, "w_up": w_up, "w_down": w_down}


EPS = 1e-06
TINY = 1e-30
STEP = 0.04
HIGH = lax.Precision.HIGHEST

@jax.custom_vjp
def low(v):
    return lax.optimization_barrier(v.astype(jnp.bfloat16)).astype(jnp.float32)

@jax.custom_vjp
def low_back(v):
    return v

def low_keep(v):
    return (low(v), None)

def low_pass(kept, grad):
    return (grad,)

def back_keep(v):
    return (v, None)

def back_low(kept, grad):
    return (low(grad),)
low.defvjp(low_keep, low_pass)
low_back.defvjp(back_keep, back_low)

def group_rows(lengths, owners, group_id):
    owned = owners == group_id
    quarter = jnp.where(owned, lengths // SHARDS, 0).astype(jnp.int32)
    entry_ids = jnp.arange(NSEQS, dtype=jnp.int32)
    earlier = entry_ids[None, :] < entry_ids[:, None]
    offset = lax.optimization_barrier(jnp.sum(jnp.where(earlier, quarter[None, :], 0), axis=1)).astype(jnp.int32)
    row_ids = jnp.arange(TOK_DEV, dtype=jnp.int32)
    inside = owned[None, :] & (offset[None, :] <= row_ids[:, None]) & (row_ids[:, None] < offset[None, :] + quarter[None, :])
    segment = lax.optimization_barrier(jnp.sum(jnp.where(inside, entry_ids[None, :], 0), axis=1)).astype(jnp.int32)
    span_rows = lax.optimization_barrier(jnp.sum(jnp.where(inside, quarter[None, :], 0), axis=1)).astype(jnp.int32)
    first_rows = lax.optimization_barrier(jnp.sum(jnp.where(inside, offset[None, :], 0), axis=1)).astype(jnp.int32)
    shard_ids = jnp.arange(SHARDS, dtype=jnp.int32)
    position = shard_ids[:, None] * span_rows[None, :] + row_ids[None, :] - first_rows[None, :]
    return (jnp.tile(segment, SHARDS), position.reshape(-1).astype(jnp.int32))

def rms_scaled(values, gain):
    return values * lax.rsqrt(lax.optimization_barrier(jnp.mean(values * values, -1, keepdims=True)) + EPS) * gain

def mix_heads(mix_table, stacked):
    return jnp.einsum('gh,gqk->hqk', mix_table, stacked, precision=HIGH)

def attend(queries, key_rows, values, segment, position, logit_mix, weight_mix):
    score_scale = HEAD_DIM ** (-0.5)
    logits = low_back(jnp.einsum('qhd,khd->hqk', queries, key_rows, precision=HIGH) * score_scale)
    mixed_logits = mix_heads(logit_mix, logits)
    visible = (segment[:, None] == segment[None, :]) & (position[None, :] <= position[:, None])
    masked = jnp.where(visible[None], mixed_logits, -jnp.inf)
    row_max = lax.optimization_barrier(jnp.max(masked, -1, keepdims=True))
    totals = jnp.log(lax.optimization_barrier(jnp.sum(jnp.exp(masked - row_max), -1, keepdims=True))) + row_max
    soft_probs = jnp.exp(masked - totals)
    weights = low(mix_heads(weight_mix, soft_probs))
    return jnp.einsum('hqk,khd->qhd', weights, values, precision=HIGH)

def forward(inputs, norm1_gain, w_qkv, mix_logits, mix_weights, w_attn_out, norm2_gain, w_up, w_down, segment, position):
    normed_in = low(rms_scaled(inputs, norm1_gain))
    projected = low(low_back(jnp.einsum('gnd,ide->igne', normed_in, low(w_qkv), precision=HIGH)))
    projected = projected.reshape(3, GROUPS, GROUP_TOK, HEADS, HEAD_DIM)

    def per_group(pieces):
        return attend(pieces[0], pieces[1], pieces[2], pieces[3], pieces[4], mix_logits, mix_weights)
    head_outs = lax.map(jax.checkpoint(per_group), (projected[0], projected[1], projected[2], segment, position))
    attn_rows = low(low_back(head_outs.reshape(GROUPS, GROUP_TOK, D)))
    residual = inputs + low_back(jnp.einsum('gnd,de->gne', attn_rows, low(w_attn_out), precision=HIGH))
    normed_mid = low(rms_scaled(residual, norm2_gain))
    up_pre = low_back(jnp.einsum('gnd,df->gnf', normed_mid, low(w_up), precision=HIGH))
    activated = low(jax.nn.gelu(up_pre, approximate=True))
    return residual + jnp.einsum('gnf,fd->gnd', activated, low(w_down), precision=HIGH)

def factored(weight, gradient):
    squares = gradient * gradient + TINY
    row_means = lax.optimization_barrier(jnp.mean(squares, -1))
    col_means = lax.optimization_barrier(jnp.mean(squares, -2))
    row_scale = lax.optimization_barrier(jnp.mean(row_means, -1, keepdims=True))
    second = row_means[..., :, None] * col_means[..., None, :] / row_scale[..., None]
    return (row_means, col_means, weight - STEP * gradient * lax.rsqrt(second))

def reference(layer_input, cotangent, seq_lengths, seq_group, norm1_gain, w_qkv, mix_logits, mix_weights, w_attn_out, norm2_gain, w_up, w_down):
    segment, position = jax.vmap(lambda group_id: group_rows(seq_lengths, seq_group, group_id))(jnp.arange(GROUPS, dtype=jnp.int32))
    inputs = layer_input.astype(jnp.float32)

    def forward_all(inputs_in, gain_one, qkv_in, logit_mix, weight_mix, out_in, gain_two, up_in, down_in):
        return forward(inputs_in, gain_one, qkv_in, logit_mix, weight_mix, out_in, gain_two, up_in, down_in, segment, position)
    result, pullback = jax.vjp(forward_all, inputs, norm1_gain, w_qkv, mix_logits, mix_weights, w_attn_out, norm2_gain, w_up, w_down)
    gradients = pullback(cotangent.astype(jnp.float32))
    input_grad, grad_norm1, grad_qkv, grad_mix_logits, grad_mix_weights, grad_attn_out, grad_norm2, grad_up, grad_down = gradients
    qkv_rows, qkv_cols, new_qkv = factored(w_qkv, grad_qkv)
    out_rows, out_cols, new_attn_out = factored(w_attn_out, grad_attn_out)
    up_rows, up_cols, new_up = factored(w_up, grad_up)
    down_rows, down_cols, new_down = factored(w_down, grad_down)
    return (result.astype(jnp.bfloat16), input_grad, grad_norm1, grad_qkv, grad_mix_logits, grad_mix_weights, grad_attn_out, grad_norm2, grad_up, grad_down, qkv_rows, qkv_cols, out_rows, out_cols, up_rows, up_cols, down_rows, down_cols, new_qkv, new_attn_out, new_up, new_down)
```

```python
import functools

import jax
import jax.numpy as jnp
from jax import lax
from jax.experimental import pallas as pl
from jax.experimental.pallas import tpu as pltpu
from jax.sharding import PartitionSpec as P

EPS = 1e-06
TINY = 1e-30
STEP = 0.04
F32 = jnp.float32
BF16 = jnp.bfloat16
HEAD_BLOCK = 6
VMEM_LIMIT = 48 * 1024 * 1024


def cost(micros):
    return pl.CostEstimate(
        flops=int(micros * 1.1e9), bytes_accessed=int(micros * 3.0e6), transcendentals=0
    )


def flip(value, axis, bit):
    size = lax.axis_size(axis)
    return lax.ppermute(value, axis, [(i, i ^ bit) for i in range(size)])


def after(value, *marks):
    return lax.optimization_barrier((value,) + marks)[0]


def dot_nn(left, right):
    return lax.dot_general(left, right, (((1,), (0,)), ((), ())), preferred_element_type=F32)


def dot_nt(left, right):
    return lax.dot_general(left, right, (((1,), (1,)), ((), ())), preferred_element_type=F32)


def dot_tn(left, right):
    return lax.dot_general(left, right, (((0,), (0,)), ((), ())), preferred_element_type=F32)


def attend_kernel(
    q_ref, k_ref, v_ref, lmix_ref, wmix_ref, qseg_ref, qpos_ref, kseg_ref, kpos_ref,
    prob_ref, head_ref, out_ref, acc_ref,
):
    step = pl.program_id(0)

    @pl.when(step == 0)
    def _():
        acc_ref[...] = jnp.zeros_like(acc_ref)

    queries = q_ref[...].astype(F32)
    keys = k_ref[...]
    values = v_ref[...]
    visible = (qseg_ref[...] == kseg_ref[...]) & (kpos_ref[...] <= qpos_ref[...])
    total = acc_ref[...]

    def product(i):
        scaled = queries * lmix_ref[i]
        high = scaled.astype(BF16)
        rest = (scaled - high.astype(F32)).astype(BF16)
        return dot_nt(high, keys) + dot_nt(rest, keys)

    ahead = product(0)
    for i in range(HEAD_BLOCK):
        mixed = jnp.where(visible, ahead, -jnp.inf)
        if i + 1 < HEAD_BLOCK:
            ahead = product(i + 1)
        top = jnp.max(mixed, -1, keepdims=True)
        raised = jnp.exp(mixed - top)
        probs = (raised * (1.0 / jnp.sum(raised, -1, keepdims=True))).astype(BF16)
        prob_ref[i] = probs
        heads = dot_nn(probs, values)
        head_ref[i] = heads.astype(BF16)
        total = total + heads * wmix_ref[i]
    acc_ref[...] = total

    @pl.when(step == pl.num_programs(0) - 1)
    def _():
        out_ref[...] = total.astype(BF16)


def attend(queries, keys, values, lmix, wmix, qseg, qpos, kseg, kpos):
    rows, width = queries.shape
    cols = keys.shape[0]
    heads = lmix.shape[0]

    def whole(shape):
        return pl.BlockSpec(shape, lambda i: (0,) * len(shape))

    def per_head(*shape):
        return pl.BlockSpec((HEAD_BLOCK,) + shape, lambda i: (i, 0, 0))

    return pl.pallas_call(
        attend_kernel,
        grid=(heads // HEAD_BLOCK,),
        in_specs=[
            whole((rows, width)),
            whole((cols, width)),
            whole((cols, width)),
            per_head(1, width),
            per_head(1, width),
            whole((rows, 1)),
            whole((rows, 1)),
            whole((1, cols)),
            whole((1, cols)),
        ],
        out_specs=[per_head(rows, cols), per_head(rows, width), whole((rows, width))],
        out_shape=[
            jax.ShapeDtypeStruct((heads, rows, cols), BF16),
            jax.ShapeDtypeStruct((heads, rows, width), BF16),
            jax.ShapeDtypeStruct((rows, width), BF16),
        ],
        scratch_shapes=[pltpu.VMEM((rows, width), F32)],
        compiler_params=pltpu.CompilerParams(vmem_limit_bytes=VMEM_LIMIT),
        cost_estimate=cost(12),
        name="attend",
    )(queries, keys, values, lmix, wmix, qseg, qpos, kseg, kpos)


def back_values_kernel(prob_ref, dao_ref, wmix_ref, dy_ref, out_ref, acc_ref):
    step = pl.program_id(0)

    @pl.when(step == 0)
    def _():
        acc_ref[...] = jnp.zeros_like(acc_ref)

    outer = dao_ref[...].astype(F32)
    scaled = [(outer * wmix_ref[i]).astype(BF16) for i in range(HEAD_BLOCK)]
    all_probs = prob_ref[...].reshape(-1, prob_ref.shape[2])
    acc_ref[...] += dot_tn(all_probs, jnp.concatenate(scaled, 0))

    @pl.when(step == pl.num_programs(0) - 1)
    def _():
        write_halves(out_ref, acc_ref[...].astype(BF16), dy_ref[...])


def write_halves(out_ref, upper, lower):
    rows = upper.shape[0]
    half = out_ref.shape[2]
    for i in range(2):
        out_ref[i, :rows] = upper[:, i * half : (i + 1) * half]
        out_ref[i, rows:] = lower[:, i * half : (i + 1) * half]


def back_values(probs, outer, wmix, grad_rows):
    heads, rows, cols = probs.shape
    width = outer.shape[1]

    def whole(shape):
        return pl.BlockSpec(shape, lambda i: (0,) * len(shape))

    def per_head(*shape):
        return pl.BlockSpec((HEAD_BLOCK,) + shape, lambda i: (i, 0, 0))

    return pl.pallas_call(
        back_values_kernel,
        grid=(heads // HEAD_BLOCK,),
        in_specs=[
            per_head(rows, cols), whole((rows, width)), per_head(1, width), whole((rows, width)),
        ],
        out_specs=whole((2, cols + rows, width // 2)),
        out_shape=jax.ShapeDtypeStruct((2, cols + rows, width // 2), BF16),
        scratch_shapes=[pltpu.VMEM((cols, width), F32)],
        compiler_params=pltpu.CompilerParams(vmem_limit_bytes=VMEM_LIMIT),
        cost_estimate=cost(4),
        name="back_values",
    )(probs, outer, wmix, grad_rows)


def attend_back_kernel(
    prob_ref, head_ref, q_ref, k_ref, v_ref, dao_ref, lmix_ref, wmix_ref,
    out_ref, lsum_ref, wsum_ref, dq_acc, dk_acc,
):
    step = pl.program_id(0)

    @pl.when(step == 0)
    def _():
        dq_acc[...] = jnp.zeros_like(dq_acc)
        dk_acc[...] = jnp.zeros_like(dk_acc)

    queries = q_ref[...].astype(F32)
    outer = dao_ref[...].astype(F32)
    keys = k_ref[...]
    values = v_ref[...]
    dq_sum = dq_acc[...]
    scaled_q = [(queries * lmix_ref[i]).astype(BF16) for i in range(HEAD_BLOCK)]
    scaled_out = [(outer * wmix_ref[i]).astype(BF16) for i in range(HEAD_BLOCK)]
    grads = []
    ahead = dot_nt(scaled_out[0], values)
    for i in range(HEAD_BLOCK):
        grad_probs = ahead
        if i + 1 < HEAD_BLOCK:
            ahead = dot_nt(scaled_out[i + 1], values)
        probs = prob_ref[i].astype(F32)
        product = probs * grad_probs
        shift = jnp.sum(product, -1, keepdims=True)
        grad_mixed = (product - probs * shift).astype(BF16)
        grads.append(grad_mixed)
        back = dot_nn(grad_mixed, keys)
        dq_sum = dq_sum + back * lmix_ref[i]
        lsum_ref[i] = jnp.sum(back * queries, 0, keepdims=True)
        wsum_ref[i] = jnp.sum(head_ref[i].astype(F32) * outer, 0, keepdims=True)
    dq_acc[...] = dq_sum
    dk_acc[...] += dot_tn(jnp.concatenate(grads, 0), jnp.concatenate(scaled_q, 0))

    @pl.when(step == pl.num_programs(0) - 1)
    def _():
        write_halves(out_ref, dk_acc[...].astype(BF16), dq_sum.astype(BF16))


def attend_back(probs, heads_out, queries, keys, values, outer, lmix, wmix):
    rows, width = queries.shape
    cols = keys.shape[0]
    heads = lmix.shape[0]
    half = width // 2

    def whole(shape):
        return pl.BlockSpec(shape, lambda i: (0,) * len(shape))

    def per_head(*shape):
        return pl.BlockSpec((HEAD_BLOCK,) + shape, lambda i: (i, 0, 0))

    return pl.pallas_call(
        attend_back_kernel,
        grid=(heads // HEAD_BLOCK,),
        in_specs=[
            per_head(rows, cols),
            per_head(rows, width),
            whole((rows, width)),
            whole((cols, width)),
            whole((cols, width)),
            whole((rows, width)),
            per_head(1, width),
            per_head(1, width),
        ],
        out_specs=[whole((2, cols + rows, half)), per_head(1, width), per_head(1, width)],
        out_shape=[
            jax.ShapeDtypeStruct((2, cols + rows, half), BF16),
            jax.ShapeDtypeStruct((heads, 1, width), F32),
            jax.ShapeDtypeStruct((heads, 1, width), F32),
        ],
        scratch_shapes=[pltpu.VMEM((rows, width), F32), pltpu.VMEM((cols, width), F32)],
        compiler_params=pltpu.CompilerParams(vmem_limit_bytes=VMEM_LIMIT),
        cost_estimate=cost(11),
        name="attend_back",
    )(probs, heads_out, queries, keys, values, outer, lmix, wmix)


def group_rows(lengths, owners, group_id, pieces, tok_dev):
    shards = pieces.shape[0]
    owned = owners == group_id
    quarter = jnp.where(owned, lengths // shards, 0)
    entry_ids = jnp.arange(lengths.shape[0], dtype=jnp.int32)
    earlier = entry_ids[None, :] < entry_ids[:, None]
    offset = jnp.sum(jnp.where(earlier, quarter[None, :], 0), axis=1)
    row_ids = jnp.arange(tok_dev, dtype=jnp.int32)
    inside = (
        owned[None, :]
        & (offset[None, :] <= row_ids[:, None])
        & (row_ids[:, None] < offset[None, :] + quarter[None, :])
    )
    segment = jnp.sum(jnp.where(inside, entry_ids[None, :], 0), axis=1)
    span_rows = jnp.sum(jnp.where(inside, quarter[None, :], 0), axis=1)
    first_rows = jnp.sum(jnp.where(inside, offset[None, :], 0), axis=1)
    position = pieces[:, None] * span_rows[None, :] + row_ids[None, :] - first_rows[None, :]
    return (jnp.tile(segment, shards), position.reshape(-1))


def rms_parts(values):
    inv_scale = lax.rsqrt(jnp.mean(values * values, -1, keepdims=True) + EPS)
    return (values * inv_scale, inv_scale)


def rms_back(grad_out, normed, inv_scale, gain):
    grad_normed = grad_out * gain
    grad_in = inv_scale * (grad_normed - normed * jnp.mean(grad_normed * normed, -1, keepdims=True))
    return grad_in


def gelu_tanh(values):
    return jax.nn.gelu(values, approximate=True)


def gather_rows(own, far):
    near = flip(jnp.concatenate([own, far], 0), "tp", 1)
    n = own.shape[0]
    return jnp.concatenate([own, near[:n], far, near[n:]], 0)


def scatter_near(partial):
    n = partial.shape[-2] // 4
    low = partial.astype(BF16)
    return flip(
        jnp.concatenate([low[..., n : 2 * n, :], low[..., 3 * n :, :]], -2), "tp", 1
    )


def scatter_far(partial, got):
    n = partial.shape[-2] // 4
    first = partial[..., 2 * n : 3 * n, :].astype(F32) + got[..., n:, :].astype(F32)
    first = first.astype(BF16)
    return first, flip(first, "tp", 2)


def scatter_sum(partial, got, back):
    n = partial.shape[-2] // 4
    own = partial[..., :n, :].astype(F32)
    return own + got[..., :n, :].astype(F32) + back.astype(F32)


def fold_near(halves, source):
    return lax.ppermute(halves, "tp", [(source, 1 - source), (2 + source, 3 - source)])


def to_chip(value, core):
    return lax.ppermute(value, "tp", [(core, 2 + core), (2 + core, core)])


def fold_kernel(far_ref, own_send, got_send, own_keep, got_keep, send_ref, keep_ref):
    rows = own_send.shape[1]
    n = rows // 5
    for own, got, out in ((own_send, got_send, send_ref), (own_keep, got_keep, keep_ref)):
        for r in range(4):
            theirs = got[0, (r ^ 1) * n : (r ^ 1) * n + n].astype(F32)
            total = own[0, r * n : r * n + n].astype(F32) + theirs
            out[r * n : r * n + n] = total.astype(out.dtype)
        out[4 * n : rows] = own[0, 4 * n :].astype(out.dtype)
        out[rows:] = got[0, 4 * n :].astype(out.dtype)


def fold(halves, got, far):
    _, rows, half = halves.shape
    total = rows + rows // 5

    def part(other):
        return pl.BlockSpec(
            (1, rows, half), lambda i, far: ((1 - far[0]) if other else far[0], 0, 0)
        )

    return pl.pallas_call(
        fold_kernel,
        grid_spec=pltpu.PrefetchScalarGridSpec(
            num_scalar_prefetch=1,
            grid=(1,),
            in_specs=[part(True), part(True), part(False), part(False)],
            out_specs=[pl.BlockSpec((total, half), lambda i, far: (0, 0))] * 2,
        ),
        out_shape=[
            jax.ShapeDtypeStruct((total, half), BF16), jax.ShapeDtypeStruct((total, half), F32),
        ],
        compiler_params=pltpu.CompilerParams(vmem_limit_bytes=VMEM_LIMIT),
        cost_estimate=cost(2),
        name="fold",
    )(far[None].astype(jnp.int32), halves, got, halves, got)


def grads_kernel(
    me_ref, k_keep, k_far, v_keep, v_far, left_ref, ao_ref, send_ref, keep_ref, cols_ref, low_ref,
):
    core = me_ref[0]
    n = left_ref.shape[0] // 4
    half = cols_ref.shape[1]

    def columns(keep, far):
        for r in range(4):
            theirs = far[(r ^ 2) * n : (r ^ 2) * n + n].astype(F32)
            cols_ref[r * n : r * n + n] = (keep[r * n : r * n + n] + theirs).astype(BF16)
        low_ref[: 2 * n] = keep[4 * n :].astype(BF16)
        low_ref[2 * n :] = far[4 * n :]

    def product(out, which, low_left):
        at = pl.ds(pl.multiple_of(which * half, 128), half)
        out[:, :half] = dot_tn(left_ref[:, at], cols_ref[...]).astype(BF16)
        out[:, half:] = dot_tn(low_left[:, at], low_ref[...]).astype(BF16)

    for which, keep, far, low_left in ((0, k_keep, k_far, left_ref), (1, v_keep, v_far, ao_ref)):

        @pl.when(core == which)
        def _():
            columns(keep, far)
            product(send_ref, 1 - me_ref[1], low_left)
            product(keep_ref, me_ref[1], low_left)


def weight_grads(core, k_keep, k_far, v_keep, v_far, normed_in, attn_rows):
    rows, width = normed_in.shape
    half = width // 2
    me = jnp.stack([core, lax.axis_index("seq") % 2]).astype(jnp.int32)
    return pl.pallas_call(
        grads_kernel,
        grid_spec=pltpu.PrefetchScalarGridSpec(
            num_scalar_prefetch=1,
            grid=(1,),
            in_specs=[
                pl.BlockSpec(v.shape, lambda i, me: (0, 0))
                for v in (k_keep, k_far, v_keep, v_far, normed_in, attn_rows)
            ],
            out_specs=[
                pl.BlockSpec((half, width), lambda i, me: (0, 0)),
                pl.BlockSpec((half, width), lambda i, me: (0, 0)),
                pl.BlockSpec((rows, half), lambda i, me: (0, 0)),
            ],
            scratch_shapes=[pltpu.VMEM((rows, half), BF16)],
        ),
        out_shape=[
            jax.ShapeDtypeStruct((half, width), BF16),
            jax.ShapeDtypeStruct((half, width), BF16),
            jax.ShapeDtypeStruct((rows, half), BF16),
        ],
        compiler_params=pltpu.CompilerParams(vmem_limit_bytes=VMEM_LIMIT),
        cost_estimate=cost(5),
        name="weight_grads",
    )(me, k_keep, k_far, v_keep, v_far, normed_in, attn_rows)


def halves_of(value, bit):
    me = (lax.axis_index("seq") // bit) % 2
    pair = value.reshape((2, -1) + value.shape[1:])
    send = lax.dynamic_index_in_dim(pair, 1 - me, 0, keepdims=False)
    return send, lax.dynamic_index_in_dim(pair, me, 0, keepdims=False)


def seq_levels():
    size = lax.axis_size("seq")
    levels = []
    bit = 2
    while bit < size:
        levels.append((bit, 2 * bit) if 2 * bit < size else (bit,))
        bit *= 4
    return levels


def offsets(bits):
    return [sum(b for i, b in enumerate(bits) if (n >> i) & 1) for n in range(1, 1 << len(bits))]


def line_swap(value):
    size = lax.axis_size("seq")
    groups = [list(range(low, size, 2)) for low in range(2)]
    return lax.all_to_all(value, "seq", 0, 0, axis_index_groups=groups, tiled=True)


def line_sum(value, *marks):
    me = lax.axis_index("seq")
    for bits in seq_levels()[::-1]:
        count = 1 << len(bits)
        blocks = value.reshape((count, -1) + value.shape[1:])

        def pick(which):
            at = sum(((which // b) % 2) << i for i, b in enumerate(bits))
            return lax.dynamic_index_in_dim(blocks, at, 0, keepdims=False)

        got = [flip(pick(me ^ off), "seq", off) for off in offsets(bits)]
        total = after(pick(me), *marks).astype(F32)
        for piece in got:
            total = total + piece.astype(F32)
        value = total.astype(BF16)
    return value


def line_gather(block):
    value, ids = block[None], [0]
    for bits in seq_levels():
        got = [flip(value, "seq", off) for off in offsets(bits)]
        ids = ids + [i ^ off for off in offsets(bits) for i in ids]
        value = jnp.concatenate([value] + got, 0)
    return value, [i // 2 for i in ids]


def all_sum(value):
    for axis in ("seq", "tp"):
        bit = 1
        while bit < lax.axis_size(axis):
            value = value + flip(value, axis, bit)
            bit *= 2
    return value


def tp_sum(value):
    for bit in (1, 2):
        value = value + flip(value, "tp", bit)
    return value


def row_vector(column):
    wide = jnp.broadcast_to(column, (column.shape[0], 128))
    return jnp.transpose(wide)[:1]


def line_rows(value, ids):
    if value.shape[1] % 16 == 0:
        return value, ids
    me = lax.axis_index("seq") // 2
    at = [ids.index(i) for i in range(len(ids))]
    order = jnp.take(jnp.array(at, jnp.int32), jnp.arange(len(ids), dtype=jnp.int32) ^ me)
    rows = jnp.take(value, order, axis=0).reshape(1, -1, value.shape[2])
    return rows.reshape((2, -1) + rows.shape[2:]), None


def spread(value, ids, *marks):
    half = value.shape[0] // 2
    over_y = flip(value, "seq", 1)
    over_x = flip(value, "tp", 2)
    over_y = after(over_y, *marks)
    sent = (over_y[:half], over_x[half:])
    corner_low = flip(sent[0], "tp", 2)
    corner_high = flip(sent[1], "seq", 1)
    low, high = (ids[:half], ids[half:]) if ids else (None, None)
    return [
        (value, ids, 0, 0, 0, 0),
        (over_y, ids, 1, 0, 0, 0),
        (over_x, ids, 0, 1, 0, 0),
        (corner_low, low, 1, 1, 0, 0),
        (corner_high, high, 1, 1, 0, half),
    ], sent


def spread_core(pieces, *marks):
    held = [after(v, *marks) if at > 2 else v for at, (v, *_) in enumerate(pieces)]
    own = [(h,) + p[1:] for h, p in zip(held, pieces)]
    return own + [(flip(v, "tp", 1), i, y, x, 1, b) for v, i, y, x, _, b in own]


def update_kernel(layout, me_ref, *refs):
    sources, (w_ref, wout_ref), outs = refs[:-11], refs[-11:-9], refs[-9:]
    me_seq, me_far, me_core = me_ref[0], me_ref[1] // 2, me_ref[1] % 2

    def update(core, part, weight, grad, new, rows, cols):
        height, width = grad.shape[1:]
        half = width // 2
        for near in range(2):

            @pl.when((me_core ^ near) == core)
            def _():
                for ref, (ids, y, x, c, first) in zip(sources, layout):
                    if c != near:
                        continue
                    col = pl.multiple_of((me_far ^ x) * half, 128)
                    top = ((me_seq % 2) ^ y) * (height // 2)
                    n = ref.shape[1]
                    for k in range(ref.shape[0]):
                        line = first + k if ids is None else (me_seq // 2) ^ ids[k]
                        at = pl.multiple_of(top + line * n, 16)
                        block = ref[k, :, part * half : (part + 1) * half]
                        grad[0, pl.ds(at, n), pl.ds(col, half)] = block.astype(F32)

        gradient = grad[0]
        squares = gradient * gradient + TINY
        row_means = jnp.sum(squares, -1, keepdims=True) * (1.0 / width)
        col_means = jnp.sum(squares, 0, keepdims=True) * (1.0 / height)
        scale = jnp.sum(row_means, 0, keepdims=True) * (1.0 / height)
        rows[0] = row_vector(row_means)
        cols[0] = col_means
        pace = lax.rsqrt(row_means / scale) * STEP
        new[0] = weight - gradient * pace * lax.rsqrt(col_means)
        return gradient

    for at, (core, part) in enumerate(((0, 1), (0, 0), (1, 0), (1, 1))):

        @pl.when(pl.program_id(0) == at)
        def _():
            if at == 3:
                update(core, part, wout_ref[0], *outs[4:8])
                return
            weight = w_ref[0]
            gradient = update(core, part, weight, *outs[:4])
            dots = weight.astype(BF16).astype(F32) * gradient
            dots = row_vector(jnp.sum(dots, -1, keepdims=True))
            outs[8][...] = dots if at == 0 else outs[8][...] + dots


def attn_update(pieces, w_qkv, w_out):
    width = w_qkv.shape[1]
    me = jnp.stack([lax.axis_index("seq"), lax.axis_index("tp")]).astype(jnp.int32)

    def whole(shape):
        return pl.BlockSpec(shape, lambda i, me: (0,) * len(shape))

    def by_step(shape):
        return pl.BlockSpec((1,) + shape, lambda i, me: (jnp.minimum(i, 2), 0, 0))

    shapes = [(width, width), (width, width), (1, width), (1, width)]
    return pl.pallas_call(
        functools.partial(update_kernel, [p[1:] for p in pieces]),
        grid_spec=pltpu.PrefetchScalarGridSpec(
            num_scalar_prefetch=1,
            grid=(4,),
            in_specs=[whole(p[0].shape) for p in pieces]
            + [by_step((width, width)), whole((1, width, width))],
            out_specs=[by_step(shape) for shape in shapes]
            + [whole((1,) + shape) for shape in shapes]
            + [whole((1, width))],
        ),
        out_shape=[jax.ShapeDtypeStruct((3,) + shape, F32) for shape in shapes]
        + [jax.ShapeDtypeStruct((1,) + shape, F32) for shape in shapes]
        + [jax.ShapeDtypeStruct((1, width), F32)],
        compiler_params=pltpu.CompilerParams(vmem_limit_bytes=VMEM_LIMIT),
        cost_estimate=cost(14),
        name="attn_update",
    )(me, *[p[0] for p in pieces], w_qkv, w_out[None])


def collect_kernel(step, me_ref, own_ref, over_ref, grad_ref, rows_ref, cols_ref):
    lines, _, n, width = own_ref.shape
    for off, ref in enumerate((own_ref, over_ref)):
        for line in range(lines):
            at = pl.multiple_of((me_ref[0] ^ off) * (lines * n if step == 1 else n), 16)
            at = at + line * step * n
            grad_ref[pl.ds(at, n)] = ref[line, 0].astype(F32)
    gradient = grad_ref[...]
    squares = gradient * gradient + TINY
    rows_ref[...] = row_vector(jnp.sum(squares, -1, keepdims=True))
    cols_ref[...] = jnp.sum(squares, 0, keepdims=True)


def collect(own, over, which, step, micros):
    me = lax.axis_index("seq") % 2
    if own.shape[2] % 16:
        pair = jnp.where(me == 0, jnp.stack([own, over]), jnp.stack([over, own]))[:, :, which]
        pair = pair if step == 1 else pair.swapaxes(0, 1)
        full = pair.reshape(2, 1, -1, own.shape[3])
        own, over, which, step, me = full[:1], full[1:], 0, 1, jnp.int32(0)
    lines, _, n, width = own.shape
    height = 2 * lines * n
    source = pl.BlockSpec((lines, 1, n, width), lambda i, me: (0, which, 0, 0))
    shapes = [(height, width), (1, height), (1, width)]
    grad, rows, cols = pl.pallas_call(
        functools.partial(collect_kernel, step),
        grid_spec=pltpu.PrefetchScalarGridSpec(
            num_scalar_prefetch=1,
            grid=(1,),
            in_specs=[source, source],
            out_specs=[pl.BlockSpec(shape, lambda i, me: (0, 0)) for shape in shapes],
        ),
        out_shape=[jax.ShapeDtypeStruct(shape, F32) for shape in shapes],
        compiler_params=pltpu.CompilerParams(vmem_limit_bytes=VMEM_LIMIT),
        cost_estimate=cost(micros),
        name="collect",
    )(me[None].astype(jnp.int32), own, over)
    return grad, rows[0], cols[0]


def per_device(
    layer_input,
    cotangent,
    seq_lengths,
    seq_group,
    norm1_gain,
    w_qkv,
    mix_logits,
    mix_weights,
    w_attn_out,
    norm2_gain,
    w_up,
    w_down,
):
    shards = lax.axis_size("tp")
    groups = lax.axis_size("seq")
    shard_id = lax.axis_index("tp")
    group_id = lax.axis_index("seq")
    tok_dev = layer_input.shape[1]
    width = layer_input.shape[2]
    half = width // 2
    head_count = mix_logits.shape[0]
    head_dim = width // head_count
    core = shard_id % 2
    far = shard_id // 2
    group_n = tok_dev * shards
    lines = groups // 2

    own_x = layer_input[0]
    far_x = flip(own_x, "tp", 2)
    pieces = shard_id ^ jnp.arange(shards, dtype=jnp.int32)
    segment, position = group_rows(seq_lengths, seq_group, group_id, pieces, tok_dev)
    lmix = jnp.repeat(mix_logits.T * head_dim**-0.5, head_dim, axis=1)[:, None, :]
    wmix = jnp.repeat(mix_weights, head_dim, axis=1)[:, None, :]
    qkv_b = w_qkv.astype(BF16)
    far_x = after(far_x, qkv_b, lmix, wmix, segment, position)
    inputs_b = gather_rows(own_x, far_x)
    own_cot = after(cotangent[0], far_x)
    far_cot = flip(own_cot, "tp", 2)

    inputs = inputs_b.astype(F32)
    normed1, inv1 = rms_parts(inputs)
    normed_in = (normed1 * norm1_gain).astype(BF16)
    normed1_own = normed1[:tok_dev]
    inv1_own = inv1[:tok_dev]
    queries = jnp.dot(normed_in[:tok_dev], qkv_b[0], preferred_element_type=F32).astype(BF16)
    keys = jnp.dot(normed_in, qkv_b[1], preferred_element_type=F32).astype(BF16)
    values = jnp.dot(normed_in, qkv_b[2], preferred_element_type=F32).astype(BF16)

    probs, heads_out, attn_own = attend(
        queries,
        keys,
        values,
        lmix,
        wmix,
        segment[:tok_dev, None],
        position[:tok_dev, None],
        segment[None, :],
        position[None, :],
    )
    far_ao = flip(attn_own, "tp", 2)
    cot_b = gather_rows(own_cot, after(far_cot, attn_own))
    out_b = after(w_attn_out, attn_own).astype(BF16)
    up_b = after(w_up, attn_own).astype(BF16)
    down_b = after(w_down, attn_own).astype(BF16)
    grad_act = jnp.einsum("nd,fd->nf", cot_b, down_b, preferred_element_type=F32)
    far_ao = after(far_ao, grad_act, out_b, up_b)
    attn_rows = gather_rows(attn_own, far_ao)

    residual = inputs + jnp.dot(attn_rows, out_b, preferred_element_type=F32)
    normed2, inv2 = rms_parts(residual)
    normed_mid = (normed2 * norm2_gain).astype(BF16)
    up_pre = jnp.dot(normed_mid, up_b, preferred_element_type=F32)
    activated, gelu_back = jax.vjp(gelu_tanh, up_pre)
    act_b = activated.astype(BF16)
    grad_up_in = gelu_back(grad_act)[0].astype(BF16)
    mid_part = jnp.einsum("nf,df->nd", grad_up_in, up_b, preferred_element_type=F32)
    mid_got = scatter_near(mid_part)
    act_b, ignored = lax.optimization_barrier((act_b, mid_part))
    grad_down = dot_tn(act_b, cot_b).astype(BF16)
    mid_got = after(mid_got, grad_down)
    mid_first, mid_back = scatter_far(mid_part, mid_got)
    grad_up = dot_tn(after(normed_mid, mid_first), grad_up_in).astype(BF16)
    down_send, down_keep = halves_of(after(grad_down, mid_first), 1)
    down_got = flip(down_send, "seq", 1)
    up_lines = line_swap(grad_up.reshape(lines, -1, width))
    mid_back = after(mid_back, grad_up)
    grad_mid = scatter_sum(mid_part, mid_got, mid_back)

    grad_res_norm = rms_back(grad_mid, normed2[:tok_dev], inv2[:tok_dev], norm2_gain)
    grad_res = own_cot.astype(F32) + grad_res_norm
    grad_res_b = grad_res.astype(BF16)
    grad_heads = dot_nt(grad_res_b, out_b).astype(BF16)
    v_halves = back_values(probs, grad_heads, wmix, grad_res_b)
    v_got = fold_near(v_halves, 0)
    down_half = (after(down_keep, v_halves).astype(F32) + down_got.astype(F32)).astype(BF16)
    k_halves, lsum, wsum = attend_back(
        probs, heads_out, queries, keys, values, after(grad_heads, v_halves, down_half), lmix, wmix
    )
    k_got = fold_near(k_halves, 1)

    v_send, v_keep = fold(v_halves, after(v_got, k_halves), far)
    v_far = to_chip(v_send, 1)
    up_sum = jnp.sum(after(up_lines, v_send).astype(F32), 0).astype(BF16)
    up_send, up_keep = halves_of(up_sum, 1)
    up_got = flip(up_send, "seq", 1)
    down_lines = line_swap(after(down_half, up_sum).reshape(lines, -1, width))
    k_send, k_keep = fold(k_halves, after(k_got, up_sum), far)
    k_far = to_chip(k_send, 0)
    branch = jnp.dot(after(act_b, k_send), down_b, preferred_element_type=F32).astype(BF16)
    down_block = jnp.sum(after(down_lines, k_send).astype(F32), 0)
    up_block = after(up_keep, k_send).astype(F32) + up_got.astype(F32)
    ffn_block = jnp.stack([down_block, up_block]).astype(BF16)
    ffn_spread = jnp.broadcast_to(ffn_block[None], (lines,) + ffn_block.shape)
    ffn_line = line_swap(ffn_spread)
    send, keep, first_cols = weight_grads(
        core, k_keep, after(k_far, ffn_spread, branch), v_keep, v_far, normed_in, attn_rows
    )
    got = flip(send, "seq", 1)

    first_w = lax.dynamic_slice(
        lax.dynamic_index_in_dim(qkv_b, 1 + core, 0, keepdims=False), (0, far * half), (width, half)
    )
    in_part = dot_nt(after(first_cols, keep), first_w)
    rows_part = jnp.stack([in_part.astype(BF16), branch])
    rows_got = scatter_near(rows_part)
    dq_own = jnp.concatenate([k_halves[0, group_n:], k_halves[1, group_n:]], 1)
    dh_own = dot_nt(after(dq_own, keep), qkv_b[0])
    rows_first, rows_back = scatter_far(rows_part, rows_got)
    grad_mix_logits = (
        jnp.sum(lsum.reshape(head_count, head_count, head_dim), -1).T * head_dim**-0.5
    )
    grad_mix_weights = jnp.sum(wsum.reshape(head_count, head_count, head_dim), -1)
    mixes = jnp.stack([grad_mix_logits, grad_mix_weights]).reshape(-1)

    mixes = after(mixes, keep)
    for axis, bit in (("tp", 2), ("tp", 1)):
        mixes = mixes + flip(mixes, axis, bit)
    half_sum = (after(keep, mixes).astype(F32) + got.astype(F32)).astype(BF16)
    mixes = after(mixes, half_sum)
    mixes = mixes + flip(mixes, "seq", 1)
    block = line_sum(half_sum, rows_first, ffn_line, mixes)
    ffn_over = flip(after(ffn_line, half_sum), "seq", 1)
    rows_sum = scatter_sum(rows_part, rows_got, after(rows_back, block))
    block_out = (rows_sum[1] + residual[:tok_dev]).astype(BF16)[None]
    grad_in_norm = rms_back(rows_sum[0] + dh_own, normed1_own, inv1_own, norm1_gain)
    input_grad = grad_res + grad_in_norm
    line, line_ids = line_rows(*line_gather(block))
    line = after(line, block_out)
    grad_down, down_rowsum, down_colsum = collect(ffn_line, after(ffn_over, block), 0, 1, 10)
    line = after(line, grad_down)
    grad_up, up_rowsum, up_colsum = collect(ffn_line, after(ffn_over, line), 1, 2, 2)
    grad_norm2 = jnp.sum(up_b.astype(F32) * grad_up, 1) / norm2_gain
    mixes = after(mixes, line)
    for bit in [2 << i for i in range(10) if 2 << i < groups]:
        mixes = mixes + flip(mixes, "seq", bit)
    shard_pieces, sent = spread(line, line_ids, grad_up, mixes)
    full_hidden = w_up.shape[1] * shards
    totals = after(tp_sum(jnp.stack([up_rowsum, down_colsum, grad_norm2])), *sent)
    up_rows = totals[0] / full_hidden
    down_cols = totals[1] / full_hidden
    grad_norm2 = totals[2]
    up_cols = up_colsum / width
    down_rows = down_rowsum / width
    up_pace = lax.rsqrt(up_rows / jnp.mean(up_rows)) * STEP
    new_up = w_up - grad_up * up_pace[:, None] * lax.rsqrt(up_cols)[None, :]
    down_pace = lax.rsqrt(down_cols / jnp.mean(down_cols)) * STEP
    new_down = w_down - grad_down * lax.rsqrt(down_rows)[:, None] * down_pace[None, :]
    shard_pieces = spread_core(shard_pieces, new_up, new_down)
    mixes = mixes.reshape(2, head_count, head_count)
    updated = attn_update(shard_pieces, w_qkv, w_attn_out)
    grad_qkv, new_qkv, qkv_rows, qkv_cols, grad_o, new_o, out_rows, out_cols, dots = updated
    grad_norm1 = dots[0] / norm1_gain
    grad_mix_logits = mixes[0]
    grad_mix_weights = mixes[1]
    return (
        block_out,
        input_grad[None],
        grad_norm1,
        grad_qkv,
        grad_mix_logits,
        grad_mix_weights,
        grad_o[0],
        grad_norm2,
        grad_up,
        grad_down,
        qkv_rows[:, 0],
        qkv_cols[:, 0],
        out_rows[0, 0],
        out_cols[0, 0],
        up_rows,
        up_cols,
        down_rows,
        down_cols,
        new_qkv,
        new_o[0],
        new_up,
        new_down,
    )


def solution(mesh):
    return jax.shard_map(
        per_device,
        mesh=mesh,
        in_specs=(
            P("seq", "tp", None),
            P("seq", "tp", None),
            P(),
            P(),
            P(),
            P(),
            P(),
            P(),
            P(),
            P(),
            P(None, "tp"),
            P("tp", None),
        ),
        out_specs=(
            P("seq", "tp", None),
            P("seq", "tp", None),
            P(),
            P(),
            P(),
            P(),
            P(),
            P(),
            P(None, "tp"),
            P("tp", None),
            P(),
            P(),
            P(),
            P(),
            P(),
            P("tp"),
            P("tp"),
            P(),
            P(),
            P(),
            P(None, "tp"),
            P("tp", None),
        ),
        check_vma=False,
    )
```
